256 devices in a mesh: seq: 32 (over y_hi, z, core), row: 8 (over x, y_lo).
Axes of the slice: x: 4, y: 4 (y_hi: 2, y_lo: 2; y = y_hi * 2 + y_lo), z: 8, core: 2. Of those that a mesh axis runs over, the one named last changes fastest.
Arguments:
- context_keys: bfloat16 [16384, 4096], P('seq', 'row'), may hold values from -6 to 6
- context_values: bfloat16 [16384, 4096], P('seq', 'row'), may hold values from -6 to 6
- question_states: bfloat16 [8192, 4096], P('seq', 'row'), may hold values from -6 to 6
- cotangent: bfloat16 [8192, 4096], P('seq', 'row'), may hold values from -6 to 6
Outputs:
- adapted: bfloat16 [8192, 4096], P('seq', 'row')
- grad_keys: bfloat16 [16384, 4096], P('seq', 'row')
- grad_values: bfloat16 [16384, 4096], P('seq', 'row')
The draws below stay inside these ranges and needn't reach their ends.
All inputs are finite; a program needn't handle non-finite values.
Results may differ from the reference program's by a relative error of at most 0.02.
Values may be sent and summed in bfloat16 or wider, within the bound.
No kernel may reach another device: no remote copies, remote signals or barrier semaphores. Data moves between devices by JAX's collectives and lax.ppermute only.
A program may use at most 64 MiB of HBM per device.

```python
import math
import jax
import jax.numpy as jnp
from jax import lax

D = 4096
TC_DEV = 512
TQ_DEV = 256
CONTEXT = 16384
QUESTIONS = 8192
N_SEQ = 32
N_ROW = 8


def strengthened(drawn, key, source, target, shards_of, factor):
    owner, partner = [(jnp.arange(drawn.shape[dim]) // (drawn.shape[dim] // shards_of)).reshape([-1 if axis == dim else 1 for axis in range(drawn.ndim)]) for dim in (source, target)]
    chosen = jax.random.permutation(key, shards_of)[partner]
    strong = (owner == chosen) | (owner == (partner + shards_of // 2) % shards_of)
    return jnp.where(strong, factor * drawn, drawn)


def level_of(stream_key, extent, cuts, low, high):
    factor_of, own = 1.0, jax.random.fold_in(stream_key, 6)
    for dim, blocks in cuts:
        heights = jnp.exp(jax.random.uniform(jax.random.fold_in(own, dim), (blocks,), jnp.float32, low / len(cuts), high / len(cuts)))
        factor_of = factor_of * jnp.repeat(heights, extent[dim] // blocks).reshape([-1 if axis == dim else 1 for axis in range(len(extent))])
    return factor_of


def normal_values(key, shape, width, reach, cuts=(), kind=jnp.bfloat16):
    values = width * jax.random.normal(key, shape, jnp.float32)
    if cuts:
        values = values * level_of(key, shape, cuts, -0.22, 0.18)
    return jnp.clip(values, -reach, reach).astype(kind)


def noise_with(key, shape, scale, limit, split, heavy, held_as=jnp.bfloat16):
    array = scale * jax.random.normal(key, shape, jnp.float32)
    if split:
        array = array * level_of(key, shape, split, -0.22, 0.18)
    return jnp.clip(strengthened(array, jax.random.fold_in(key, 3), *heavy), -limit, limit).astype(held_as)


def setup_inputs(seed: int = 0) -> dict:
    keys = jax.random.split(jax.random.key(seed), 5)
    return {
        "context_keys": normal_values(keys[0], (CONTEXT, D), 1.0, 6.0, ((0, 32), (1, 8))),
        "context_values": noise_with(keys[1], (CONTEXT, D), 1.0, 6.0, ((0, 32), (1, 8)), (0, 1, 32, 2.75)),
        "question_states": normal_values(keys[2], (QUESTIONS, D), 1.0, 6.0, ((0, 32), (1, 8))),
        "cotangent": noise_with(keys[3], (QUESTIONS, D), 1.0, 6.0, ((0, 32), (1, 8)), (0, 1, 32, 2.75)),
    }


def product(left, right):
    return jnp.dot(left.astype(jnp.float32), right.astype(jnp.float32), precision=lax.Precision.HIGHEST)

def block_sum(lefts, rights, scale):

    def add_block(total, pair):
        left, right = pair
        partial_value = (scale * product(left.T, right)).astype(jnp.bfloat16)
        partial_value = lax.optimization_barrier(partial_value)
        return (total + partial_value.astype(jnp.float32), None)
    start = jnp.zeros((lefts.shape[2], rights.shape[2]), jnp.float32)
    total, unused = lax.scan(add_block, start, (lefts, rights))
    return total.astype(jnp.bfloat16)

def reference(context_keys, context_values, question_states, cotangent):
    factor = 1.0 / math.sqrt(D * CONTEXT)
    adapter = block_sum(context_keys.reshape(N_SEQ, TC_DEV, D), context_values.reshape(N_SEQ, TC_DEV, D), factor)
    grad_adapter = block_sum(question_states.reshape(N_SEQ, TQ_DEV, D), cotangent.reshape(N_SEQ, TQ_DEV, D), 1.0)
    row_block = D // N_ROW
    adapted = jnp.zeros((QUESTIONS, D), jnp.float32)
    grad_values = jnp.zeros((CONTEXT, D), jnp.float32)
    for position in range(N_ROW):
        lower = position * row_block
        upper = lower + row_block
        term_one = product(question_states[:, lower:upper], adapter[lower:upper]).astype(jnp.bfloat16)
        term_one = lax.optimization_barrier(term_one)
        adapted = adapted + term_one.astype(jnp.float32)
        term_two = (factor * product(context_keys[:, lower:upper], grad_adapter[lower:upper])).astype(jnp.bfloat16)
        term_two = lax.optimization_barrier(term_two)
        grad_values = grad_values + term_two.astype(jnp.float32)
    grad_keys = (factor * product(context_values, grad_adapter.T)).astype(jnp.bfloat16)
    return (adapted.astype(jnp.bfloat16), grad_keys, grad_values.astype(jnp.bfloat16))
```

```python
import math

import jax
import jax.numpy as jnp
from jax import lax
from jax.sharding import Mesh
from jax.sharding import PartitionSpec as P

SEQ = ("yh", "z", "c")
ROW = ("x", "yl")
Y = ("yh", "yl")
BF = jnp.bfloat16
F32 = jnp.float32


def ring(axis, step):
    n = lax.axis_size(axis)
    return [(i, (i + step) % n) for i in range(n)]


def passed(a, axis, step=1):
    return lax.ppermute(a, axis, ring(axis, step))


def everyone(a, axis):
    n = lax.axis_size(axis)
    return lax.all_to_all(jnp.broadcast_to(a[None], (n, *a.shape)), axis, 0, 0, tiled=True)


def sum_arrived(pieces, axis):
    arrived = lax.all_to_all(pieces, axis, 0, 0, tiled=True)
    return arrived.astype(F32).sum(axis=0)


def ordered(own, other, index):
    first = index == 0
    return jnp.stack([jnp.where(first, own, other), jnp.where(first, other, own)])


def columns_to_quarters(a, yh, c):
    t, w = a.shape[0], a.shape[1] // 4
    q = a.reshape(t, 2, 2, w)
    first = c == 0
    keep = jnp.where(first, q[:, :, 0], q[:, :, 1])
    give = jnp.where(first, q[:, :, 1], q[:, :, 0])
    both = jnp.stack([keep, passed(give, "c")])
    first = yh == 0
    keep = jnp.where(first, both[:, :, 0], both[:, :, 1])
    give = jnp.where(first, both[:, :, 1], both[:, :, 0])
    got = passed(give, "yh")
    return jnp.moveaxis(ordered(keep, got, yh), 0, 1)


def quarters_to_columns(a, yh, c):
    first = yh == 0
    keep = jnp.where(first, a[:, 0], a[:, 1])
    give = jnp.where(first, a[:, 1], a[:, 0])
    both = ordered(keep, passed(give, "yh"), yh)
    own = both[:, 0]
    whole = ordered(own, passed(both[:, 1], "c"), c)
    return jnp.moveaxis(whole, (1, 0), (1, 2)).reshape(a.shape[2], -1)


def plane_rows(a):
    own = everyone(a, Y).reshape(2, 2, *a.shape)
    return jnp.stack([own, passed(own, "c")])


def reduce_scatter_z(a, z):
    n = a.shape[0] // 8
    h = n // 2

    def chunk(k):
        return lax.dynamic_slice_in_dim(a, ((z + k) % 8) * n, n, 0)

    far = chunk(4)
    up, down = passed(far[:h], "z", 1), passed(far[h:], "z", -1)
    c = chunk(3)
    up = jnp.concatenate([c[:h] + up, c[h:]])
    c = chunk(-3)
    down = jnp.concatenate([c[:h], c[h:] + down])
    for k in (3, 2, 1):
        up, down = passed(up, "z", 1), passed(down, "z", -1)
        if k > 1:
            up, down = up + chunk(k - 1), down + chunk(1 - k)
    return (chunk(0).astype(F32) + up.astype(F32) + down.astype(F32)).astype(a.dtype)


def all_gather_z(a, z):
    n = a.shape[0]
    h = n // 2
    up, down = a, a
    found = {0: a}
    for k in (1, 2, 3):
        up, down = passed(up, "z", 1), passed(down, "z", -1)
        found[-k], found[k] = up, down
    found[4] = jnp.concatenate([passed(up[:h], "z", 1), passed(down[h:], "z", -1)])
    whole = jnp.zeros((8 * n, a.shape[1]), a.dtype)
    for k, piece in found.items():
        whole = lax.dynamic_update_slice_in_dim(whole, piece, ((z + k) % 8) * n, 0)
    return whole


def per_device(context_keys, context_values, question_states, cotangent):
    yh, z, c = (lax.axis_index(a) for a in SEQ)
    seq_count = lax.axis_size(SEQ)
    tokens, width = context_keys.shape
    factor = 1.0 / math.sqrt(width * lax.axis_size(ROW) * tokens * seq_count)
    w = width // 4

    cot = everyone(columns_to_quarters(cotangent, yh, c), "x")
    que = plane_rows(question_states)
    grad = jnp.einsum("cyltf,xcytg->lfxg", que, cot, preferred_element_type=F32)
    grad = grad.astype(BF).reshape(2 * width, 4 * w)
    grad = reduce_scatter_z(grad, z)

    val = everyone(columns_to_quarters(context_values, yh, c), "x")
    key = plane_rows(context_keys)
    adapter = factor * jnp.einsum("cyltf,xcytg->lfxg", key, val, preferred_element_type=F32)
    adapter = adapter.astype(BF).reshape(2 * width, 4 * w)
    adapter = reduce_scatter_z(adapter, z)

    grad = all_gather_z(grad, z).reshape(2, width, 4, w)
    adapter = all_gather_z(adapter, z).reshape(2, width, 4, w)

    part = factor * jnp.einsum("cyltf,lfxg->xcytg", key, grad, preferred_element_type=F32)
    grad_values = sum_arrived(part.astype(BF), "x").astype(BF)
    grad_values = quarters_to_columns(grad_values, yh, c)

    part = factor * jnp.einsum("xcytg,lfxg->cyltf", val, grad, preferred_element_type=F32)
    part = part.astype(BF)
    part = (part[0].astype(F32) + passed(part[1], "c").astype(F32)).astype(BF)
    grad_keys = sum_arrived(part.reshape(4, tokens, width), Y).astype(BF)

    part = jnp.einsum("cyltf,lfxg->xcytg", que, adapter, preferred_element_type=F32)
    adapted = sum_arrived(part.astype(BF), "x").astype(BF)
    adapted = quarters_to_columns(adapted, yh, c)
    return adapted, grad_keys, grad_values


def solution(mesh):
    split = Mesh(mesh.devices.reshape(2, 8, 2, 4, 2), SEQ + ROW)
    spec = P(SEQ, ROW)
    return jax.shard_map(
        per_device,
        mesh=split,
        in_specs=(spec, spec, spec, spec),
        out_specs=(spec, spec, spec),
        check_vma=False,
    )
```

```python
import math

import jax
import jax.numpy as jnp
from jax import lax
from jax.sharding import Mesh
from jax.sharding import PartitionSpec as P

SEQ = ("yh", "z", "c")
ROW = ("x", "yl")
Y = ("yh", "yl")
BF = jnp.bfloat16
F32 = jnp.float32


def swapped(a, axis):
    return lax.ppermute(a, axis, [(0, 1), (1, 0)])


def along_z(a, sign, cores=(0, 1)):
    n = lax.axis_size("z")
    pairs = [
        (2 * i + c, 2 * ((i + sign * (1 - 2 * c)) % n) + c) for i in range(n) for c in cores
    ]
    return lax.ppermute(a, ("z", "c"), pairs)


def everyone(a, axis):
    n = lax.axis_size(axis)
    return lax.all_to_all(jnp.broadcast_to(a[None], (n, *a.shape)), axis, 0, 0, tiled=True)


def sum_arrived(pieces, axis):
    arrived = lax.all_to_all(pieces, axis, 0, 0, tiled=True)
    return arrived.astype(F32).sum(axis=0)


def ordered(own, other, index):
    first = index == 0
    return jnp.stack([jnp.where(first, own, other), jnp.where(first, other, own)])


def chosen(blocks, index):
    out = blocks[-1]
    for i in range(len(blocks) - 2, -1, -1):
        out = jnp.where(index == i, blocks[i], out)
    return out


def places(core, z, yl):
    sign = 1 - 2 * core
    late = (yl + z + 1) % 2
    one = (z + sign * (1 + late)) % 8
    two = jnp.where(late == 0, z + 3 * sign, z + 4 * (1 - core)) % 8
    return one // 2, two // 2


def by_core(a, z, c, yl):
    blocks = jnp.split(a, 4, axis=1)

    def rows_of(core):
        return jnp.concatenate([chosen(blocks, p) for p in places(core, z, yl)], axis=1)

    return jnp.stack([rows_of(c), swapped(rows_of(1 - c), "c")])


def by_half(a, yh):
    left, right = jnp.split(a, 2, axis=1)
    first = yh == 0
    got = swapped(jnp.where(first, right, left), "yh")
    return ordered(jnp.where(first, left, right), got, yh)


def with_other_core(a):
    return jnp.stack([a, swapped(a, "c")])


def whole_columns(a, yh):
    first = yh == 0
    keep, give = jnp.where(first, a[0], a[1]), jnp.where(first, a[1], a[0])
    got = swapped(give, "yh")
    return jnp.concatenate([jnp.where(first, keep, got), jnp.where(first, got, keep)], axis=1)


def reduce_scatter_z(a, z, c):
    early = lax.dynamic_index_in_dim(a, (z + 1) % 2, 0, keepdims=False)
    late = lax.dynamic_index_in_dim(a, z % 2, 0, keepdims=False)
    sent = along_z(late[1], 1, (0,))
    sent = along_z(sent + early[1], 1)
    sent = along_z(sent + late[0], 1)
    sent = along_z(sent + early[0], 1)
    mine = jnp.where(c == 0, sent, sent + late[1])
    return (mine.astype(F32) + swapped(mine, "c").astype(F32)).astype(a.dtype)


def all_gather_z(a, z, c):
    one = along_z(a, -1)
    two = along_z(one, -1)
    three = along_z(two, -1)
    four = along_z(three, -1, (0,))
    four = jnp.where(c == 0, four, a)
    even = z % 2 == 0
    rows = [
        [jnp.where(even, two, one), jnp.where(even, four, three)],
        [jnp.where(even, one, two), jnp.where(even, three, four)],
    ]
    return jnp.stack([jnp.stack(r) for r in rows])


def per_device(context_keys, context_values, question_states, cotangent):
    yh, z, c = (lax.axis_index(a) for a in SEQ)
    yl = lax.axis_index("yl")
    tokens, width = context_keys.shape
    factor = 1.0 / math.sqrt(width * lax.axis_size(ROW) * tokens * lax.axis_size(SEQ))
    half = width // 2
    n = width // 4

    key = by_core(context_keys, z, c, yl)
    key = lax.all_gather(key, Y, axis=0, tiled=False).reshape(2, 2, *key.shape)
    que = by_core(question_states, z, c, yl)
    que = everyone(que, Y).reshape(2, 2, *que.shape)
    cot = with_other_core(everyone(by_half(cotangent, yh), "x"))
    val = with_other_core(everyone(by_half(context_values, yh), "x"))

    grad = jnp.einsum("hlctf,cxhtg->lfxg", que, cot, preferred_element_type=F32)
    grad = grad.astype(BF).reshape(2, 2, n, 4 * half)
    grad = reduce_scatter_z(grad, z, c)
    adapter = factor * jnp.einsum("hlctf,cxhtg->lfxg", key, val, preferred_element_type=F32)
    adapter = adapter.astype(BF).reshape(2, 2, n, 4 * half)
    adapter = reduce_scatter_z(adapter, z, c)

    grad = all_gather_z(grad, z, c).reshape(2, half, 4, half)
    adapter = all_gather_z(adapter, z, c).reshape(2, half, 4, half)

    def cores_summed(part):
        return (part[0].astype(F32) + swapped(part[1], "c").astype(F32)).astype(BF)

    part = factor * jnp.einsum("hlctf,lfxg->cxhtg", key, grad, preferred_element_type=F32)
    grad_values = sum_arrived(cores_summed(part.astype(BF)), "x").astype(BF)
    grad_values = whole_columns(grad_values, yh)

    part = factor * jnp.einsum("cxhtg,lfxg->hlctf", val, grad, preferred_element_type=F32)
    part = part.astype(BF).reshape(4, 2 * tokens, half)
    part = lax.psum_scatter(part, Y, scatter_dimension=0, tiled=False).reshape(2, tokens, half)
    blocks = jnp.split(part[0], 2, axis=1) + jnp.split(swapped(part[1], "c"), 2, axis=1)
    found = places(c, z, yl) + places(1 - c, z, yl)
    columns = []
    for i in range(4):
        out = blocks[3]
        for j in range(3):
            out = jnp.where(found[j] == i, blocks[j], out)
        columns.append(out)
    grad_keys = jnp.concatenate(columns, axis=1)

    part = jnp.einsum("hlctf,lfxg->cxhtg", que, adapter, preferred_element_type=F32)
    adapted = sum_arrived(cores_summed(part.astype(BF)), "x").astype(BF)
    adapted = whole_columns(adapted, yh)
    return adapted, grad_keys, grad_values


def solution(mesh):
    split = Mesh(mesh.devices.reshape(2, 8, 2, 4, 2), SEQ + ROW)
    spec = P(SEQ, ROW)
    return jax.shard_map(
        per_device,
        mesh=split,
        in_specs=(spec, spec, spec, spec),
        out_specs=(spec, spec, spec),
        check_vma=False,
    )
```

```python
import math

import jax
import jax.numpy as jnp
from jax import lax
from jax.experimental import pallas as pl
from jax.experimental.pallas import tpu as pltpu
from jax.sharding import Mesh
from jax.sharding import PartitionSpec as P

SEQ = ("yh", "z", "c")
ROW = ("x", "yl")
Y = ("yh", "yl")
BF = jnp.bfloat16
F32 = jnp.float32


def swapped(a, axis):
    return lax.ppermute(a, axis, [(0, 1), (1, 0)])


def along_z(a, sign, cores=(0, 1)):
    n = lax.axis_size("z")
    pairs = [
        (2 * i + c, 2 * ((i + sign * (1 - 2 * c)) % n) + c) for i in range(n) for c in cores
    ]
    return lax.ppermute(a, ("z", "c"), pairs)


def exchanged(pieces, axis):
    return [pieces[0]] + [
        lax.ppermute(pieces[r], axis, [(i, i ^ r) for i in range(4)]) for r in (1, 2, 3)
    ]


def chosen(blocks, index):
    out = blocks[-1]
    for i in range(len(blocks) - 2, -1, -1):
        out = jnp.where(index == i, blocks[i], out)
    return out


def places(core, z, yl):
    sign = 1 - 2 * core
    late = (yl + z + 1) % 2
    one = (z + sign * (1 + late)) % 8
    two = jnp.where(late == 0, z + 3 * sign, z + 4 * (1 - core)) % 8
    return one // 2, two // 2


def rows_of(a, core, z, yl):
    blocks = jnp.split(a, 4, axis=-1)
    return jnp.concatenate([chosen(blocks, p) for p in places(core, z, yl)], axis=-1)


def by_half(a, yh):
    left, right = jnp.split(a, 2, axis=1)
    first = yh == 0
    got = swapped(jnp.where(first, right, left), "yh")
    return jnp.where(first, left, right), got


def whole_columns(a, yh):
    got = swapped(a[1], "yh")
    first = yh == 0
    return jnp.concatenate([jnp.where(first, a[0], got), jnp.where(first, got, a[0])], axis=1)


def reduce_scatter_z(a, place, c):
    early = lax.dynamic_index_in_dim(a, (place + 1) % 2, 0, keepdims=False)
    late = lax.dynamic_index_in_dim(a, place % 2, 0, keepdims=False)
    sent = yield along_z(late[1], 1, (0,))
    for chunk in (early[1], late[0], early[0]):
        sent = yield along_z(sent + chunk, 1)
    mine = jnp.where(c == 0, sent, sent + late[1])
    yield (mine.astype(F32) + swapped(mine, "c").astype(F32)).astype(a.dtype)


def all_gather_z(a, place, c):
    found, last = [], a
    for k in range(4):
        last = yield along_z(last, -1, (0, 1) if k < 3 else (0,))
        found.append(last)
    one, two, three, four = found
    four = jnp.where(c == 0, four, a)
    even = place % 2 == 0
    rows = [
        [jnp.where(even, two, one), jnp.where(even, four, three)],
        [jnp.where(even, one, two), jnp.where(even, three, four)],
    ]
    yield jnp.stack([jnp.stack(r) for r in rows])


def tied(*arrays):
    return lax.optimization_barrier(arrays)


def added(pieces):
    return sum(p.astype(F32) for p in pieces).astype(BF)


def called(body, ins, outs):
    space = pl.BlockSpec(memory_space=pltpu.VMEM)
    return pl.pallas_call(
        body,
        out_shape=[jax.ShapeDtypeStruct(shape, BF) for shape in outs],
        in_specs=[space] * len(ins),
        out_specs=[space] * len(outs),
        compiler_params=pltpu.CompilerParams(vmem_limit_bytes=40 * 2**20),
    )(*ins)


def side_by_side(ref, h):
    return jnp.concatenate([ref[x, h] for x in range(4)], axis=1)


def outer(left, right, factor):
    f, g = left[0].shape[2], right[0].shape[3]

    def body(*refs):
        lefts, rights, out = refs[:4], refs[4:6], refs[6]
        total = [0.0, 0.0]
        for core in range(2):
            for h in range(2):
                wide = side_by_side(rights[core], h)
                for l in range(2):
                    total[l] += lax.dot_general(
                        lefts[2 * h + l][core], wide, (((0,), (0,)), ((), ())),
                        preferred_element_type=F32,
                    )
        for l in range(2):
            done = (total[l] * factor).astype(BF)
            out[l, 0], out[l, 1] = done[: f // 2], done[f // 2 :]

    return called(body, (*left, *right), [(2, 2, f // 2, 4 * g)])[0]


def through(left, middle, g, factor):
    t = left[0].shape[1]

    def body(*refs):
        lefts, mid, outs = refs[:4], refs[4], refs[5:]
        for h in range(2):
            for core in range(2):
                new = sum(
                    jnp.dot(lefts[2 * h + l][core], mid[l], preferred_element_type=F32)
                    for l in range(2)
                )
                new = (new * factor).astype(BF)
                for x in range(4):
                    outs[core][x, h] = new[:, x * g : (x + 1) * g]

    return called(body, (*left, middle), [(4, 2, t, g)] * 2)


def back(right, middle, factor):
    t, f = right[0].shape[2], middle.shape[1]

    def body(*refs):
        rights, mid, outs = refs[:2], refs[2], refs[3:]
        for core in range(2):
            for h in range(2):
                wide = side_by_side(rights[core], h)
                for l in range(2):
                    new = lax.dot_general(
                        wide, mid[l], (((1,), (1,)), ((), ())), preferred_element_type=F32
                    )
                    outs[2 * h + l][core] = (new * factor).astype(BF)

    return called(body, (*right, middle), [(2, t, f)] * 4)


def per_device(context_keys, context_values, question_states, cotangent):
    yh, z, c = (lax.axis_index(a) for a in SEQ)
    yl = lax.axis_index("yl")
    tokens, width = context_keys.shape
    factor = 1.0 / math.sqrt(width * lax.axis_size(ROW) * tokens * lax.axis_size(SEQ))
    half = width // 2
    place = z + yl
    def from_all(a):
        return lax.all_to_all(jnp.broadcast_to(a[None], (4, *a.shape)), "x", 0, 0, tiled=True)

    right = jnp.stack(by_half(jnp.concatenate([context_values, cotangent]), yh))
    left = jnp.concatenate([context_keys, question_states])
    left = jnp.stack([rows_of(left, c, z, yl), swapped(rows_of(left, 1 - c, z, yl), "c")])
    right, left = tied(right, left)
    cot = from_all(right[:, tokens:])
    que = exchanged([left[:, tokens:]] * 4, Y)
    key = exchanged([tied(left[:, :tokens], que[1])[0]] * 4, Y)
    cot, *que = tied(cot, *que)
    val = from_all(tied(right[:, :tokens], cot)[0])
    cot = cot, swapped(cot, "c")

    steps = reduce_scatter_z(outer(que, cot, 1.0), place, c)
    at, *key = tied(next(steps), *key)
    at, val = tied(steps.send(at), val)
    at, other = tied(steps.send(at), swapped(val, "c"))
    val = val, other
    at, adapter = tied(steps.send(at), outer(key, val, factor))
    grad = steps.send(at)

    steps, others = reduce_scatter_z(adapter, place, c), all_gather_z(grad, place, c)
    at, beside = tied(next(steps), next(others))
    for _ in range(3):
        at, beside = tied(steps.send(at), others.send(beside))
    adapter, grad = steps.send(at), others.send(beside).reshape(2, half, 4 * half)

    def cores_summed(own, give):
        return added((own, swapped(give, "c")))

    steps = all_gather_z(adapter, place, c)
    own, give = through(key, grad, half, factor)
    grad, give = tied(grad, give)
    at, own, *part = tied(next(steps), own, *back(val, grad, factor))
    part = exchanged(part, Y)
    at, values = tied(steps.send(at), cores_summed(own, give))
    values = lax.all_to_all(values, "x", 0, 0, tiled=True)
    at = steps.send(at)
    at, values, *part = tied(steps.send(at), values, *part)
    adapter = steps.send(at).reshape(2, half, 4 * half)
    states = cores_summed(*through(que, adapter, half, 1.0))
    part = tied(*part, states)[:4]
    states = lax.all_to_all(states, "x", 0, 0, tiled=True)
    part = added(part)
    grad_values = whole_columns(added(values), yh)

    blocks = jnp.split(part[0], 2, axis=1) + jnp.split(swapped(part[1], "c"), 2, axis=1)
    found = places(c, z, yl) + places(1 - c, z, yl)
    columns = []
    for i in range(4):
        out = blocks[3]
        for j in range(3):
            out = jnp.where(found[j] == i, blocks[j], out)
        columns.append(out)
    grad_keys = jnp.concatenate(columns, axis=1)
    adapted = whole_columns(added(states), yh)
    return adapted, grad_keys, grad_values


def solution(mesh):
    split = Mesh(mesh.devices.reshape(2, 8, 2, 4, 2), SEQ + ROW)
    spec = P(SEQ, ROW)
    return jax.shard_map(
        per_device,
        mesh=split,
        in_specs=(spec, spec, spec, spec),
        out_specs=(spec, spec, spec),
        check_vma=False,
    )
```

```python
import math

import jax
import jax.numpy as jnp
from jax import lax
from jax.experimental import pallas as pl
from jax.experimental.pallas import tpu as pltpu
from jax.sharding import Mesh
from jax.sharding import PartitionSpec as P

SEQ = ("yh", "z", "c")
ROW = ("x", "yl")
Y = ("yh", "yl")
BF = jnp.bfloat16
F32 = jnp.float32


def swapped(a, axis):
    return lax.ppermute(a, axis, [(0, 1), (1, 0)])


def along_z(a, sign, cores=(0, 1)):
    n = lax.axis_size("z")
    pairs = [
        (2 * i + c, 2 * ((i + sign * (1 - 2 * c)) % n) + c) for i in range(n) for c in cores
    ]
    return lax.ppermute(a, ("z", "c"), pairs)


def exchanged(pieces, axis):
    return [pieces[0]] + [
        lax.ppermute(pieces[r], axis, [(i, i ^ r) for i in range(4)]) for r in (1, 2, 3)
    ]


def chosen(blocks, index):
    out = blocks[-1]
    for i in range(len(blocks) - 2, -1, -1):
        out = jnp.where(index == i, blocks[i], out)
    return out


def places(core, z, yl):
    sign = 1 - 2 * core
    late = (yl + z + 1) % 2
    one = (z + sign * (1 + late)) % 8
    two = jnp.where(late == 0, z + 3 * sign, z + 4 * (1 - core)) % 8
    return one // 2, two // 2


def rows_of(a, core, z, yl):
    blocks = jnp.split(a, 4, axis=-1)
    return jnp.concatenate([chosen(blocks, p) for p in places(core, z, yl)], axis=-1)


def by_half(a, yh):
    left, right = jnp.split(a, 2, axis=1)
    first = yh == 0
    got = swapped(jnp.where(first, right, left), "yh")
    return jnp.where(first, left, right), got


def whole_columns(a, yh):
    got = swapped(a[1], "yh")
    first = yh == 0
    return jnp.concatenate([jnp.where(first, a[0], got), jnp.where(first, got, a[0])], axis=1)


def reduce_scatter_z(a, place, c):
    early = lax.dynamic_index_in_dim(a, (place + 1) % 2, 0, keepdims=False)
    late = lax.dynamic_index_in_dim(a, place % 2, 0, keepdims=False)
    sent = yield along_z(late[1], 1, (0,))
    for chunk in (early[1], late[0], early[0]):
        sent = yield along_z(sent + chunk, 1)
    mine = jnp.where(c == 0, sent, sent + late[1])
    yield (mine.astype(F32) + swapped(mine, "c").astype(F32)).astype(a.dtype)


def all_gather_z(a, place, c):
    found, last = [], a
    for k in range(4):
        last = yield along_z(last, -1, (0, 1) if k < 3 else (0,))
        found.append(last)
    one, two, three, four = found
    four = jnp.where(c == 0, four, a)
    even = place % 2 == 0
    rows = [
        [jnp.where(even, two, one), jnp.where(even, four, three)],
        [jnp.where(even, one, two), jnp.where(even, three, four)],
    ]
    yield jnp.stack([jnp.stack(r) for r in rows])


def tied(*arrays):
    return lax.optimization_barrier(arrays)


def added(pieces):
    return sum(p.astype(F32) for p in pieces).astype(BF)


def called(body, ins, outs):
    space = pl.BlockSpec(memory_space=pltpu.VMEM)
    return pl.pallas_call(
        body,
        out_shape=[jax.ShapeDtypeStruct(shape, BF) for shape in outs],
        in_specs=[space] * len(ins),
        out_specs=[space] * len(outs),
        compiler_params=pltpu.CompilerParams(vmem_limit_bytes=40 * 2**20),
    )(*ins)


def side_by_side(ref, h):
    return jnp.concatenate([ref[x, h] for x in range(4)], axis=1)


def outer(left, right, factor):
    f, g = left[0].shape[2], right[0].shape[3]

    def body(*refs):
        lefts, rights, out = refs[:4], refs[4:6], refs[6]
        total = [0.0, 0.0]
        for core in range(2):
            for h in range(2):
                wide = side_by_side(rights[core], h)
                for l in range(2):
                    total[l] += lax.dot_general(
                        lefts[2 * h + l][core], wide, (((0,), (0,)), ((), ())),
                        preferred_element_type=F32,
                    )
        for l in range(2):
            done = (total[l] * factor).astype(BF)
            out[l, 0], out[l, 1] = done[: f // 2], done[f // 2 :]

    return called(body, (*left, *right), [(2, 2, f // 2, 4 * g)])[0]


def through(left, middle, g, factor):
    t = left[0].shape[1]

    def body(*refs):
        lefts, mid, outs = refs[:4], refs[4], refs[5:]
        for h in range(2):
            for core in range(2):
                new = sum(
                    jnp.dot(lefts[2 * h + l][core], mid[l], preferred_element_type=F32)
                    for l in range(2)
                )
                new = (new * factor).astype(BF)
                for x in range(4):
                    outs[core][x, h] = new[:, x * g : (x + 1) * g]

    return called(body, (*left, middle), [(4, 2, t, g)] * 2)


def back(right, middle, factor):
    t, f = right[0].shape[2], middle.shape[1]

    def body(*refs):
        rights, mid, outs = refs[:2], refs[2], refs[3:]
        for core in range(2):
            for h in range(2):
                wide = side_by_side(rights[core], h)
                for l in range(2):
                    new = lax.dot_general(
                        wide, mid[l], (((1,), (1,)), ((), ())), preferred_element_type=F32
                    )
                    outs[2 * h + l][core] = (new * factor).astype(BF)

    return called(body, (*right, middle), [(2, t, f)] * 4)


def per_device(context_keys, context_values, question_states, cotangent):
    yh, z, c = (lax.axis_index(a) for a in SEQ)
    yl = lax.axis_index("yl")
    tokens, width = context_keys.shape
    factor = 1.0 / math.sqrt(width * lax.axis_size(ROW) * tokens * lax.axis_size(SEQ))
    half = width // 2
    place = z + yl
    def from_all(a):
        return lax.all_to_all(jnp.broadcast_to(a[None], (4, *a.shape)), "x", 0, 0, tiled=True)

    cot = jnp.stack(by_half(cotangent, yh))
    left = jnp.concatenate([context_keys, question_states])
    left = jnp.stack([rows_of(left, c, z, yl), swapped(rows_of(left, 1 - c, z, yl), "c")])
    cot, left = tied(cot, left)
    right = jnp.stack(by_half(tied(context_values, cot)[0], yh))
    cot = from_all(cot)
    que = exchanged([left[:, tokens:]] * 4, Y)
    key = exchanged([tied(left[:, :tokens], que[1])[0]] * 4, Y)
    cot, *que = tied(cot, *que)
    val = from_all(tied(right, cot)[0])
    cot = cot, swapped(cot, "c")

    steps = reduce_scatter_z(outer(que, cot, 1.0), place, c)
    at, *key = tied(next(steps), *key)
    at, val = tied(steps.send(at), val)
    at, other = tied(steps.send(at), swapped(val, "c"))
    val = val, other
    at, adapter = tied(steps.send(at), outer(key, val, factor))
    grad = steps.send(at)

    steps, others = reduce_scatter_z(adapter, place, c), all_gather_z(grad, place, c)
    at, beside = tied(next(steps), next(others))
    for _ in range(3):
        at, beside = tied(steps.send(at), others.send(beside))
    adapter, grad = steps.send(at), others.send(beside).reshape(2, half, 4 * half)

    def cores_summed(own, give):
        return added((own, swapped(give, "c")))

    steps = all_gather_z(adapter, place, c)
    own, give = through(key, grad, half, factor)
    grad, give = tied(grad, give)
    at, own, *part = tied(next(steps), own, *back(val, grad, factor))
    part = exchanged(part, Y)
    values = cores_summed(own, give)
    at = tied(steps.send(at), values)[0]
    values = lax.all_to_all(values, "x", 0, 0, tiled=True)
    at, part[2] = tied(steps.send(at), part[2])
    at, values, part[1], part[3] = tied(steps.send(at), values, part[1], part[3])
    adapter = steps.send(at).reshape(2, half, 4 * half)
    states = cores_summed(*through(que, adapter, half, 1.0))
    part = tied(*part, states)[:4]
    states = lax.all_to_all(states, "x", 0, 0, tiled=True)
    part = added(part)
    grad_values = whole_columns(added(values), yh)

    blocks = jnp.split(part[0], 2, axis=1) + jnp.split(swapped(part[1], "c"), 2, axis=1)
    found = places(c, z, yl) + places(1 - c, z, yl)
    columns = []
    for i in range(4):
        out = blocks[3]
        for j in range(3):
            out = jnp.where(found[j] == i, blocks[j], out)
        columns.append(out)
    grad_keys = jnp.concatenate(columns, axis=1)
    adapted = whole_columns(added(states), yh)
    return adapted, grad_keys, grad_values


def solution(mesh):
    split = Mesh(mesh.devices.reshape(2, 8, 2, 4, 2), SEQ + ROW)
    spec = P(SEQ, ROW)
    return jax.shard_map(
        per_device,
        mesh=split,
        in_specs=(spec, spec, spec, spec),
        out_specs=(spec, spec, spec),
        check_vma=False,
    )
```

```python
import math

import jax
import jax.numpy as jnp
from jax import lax
from jax.experimental import pallas as pl
from jax.experimental.pallas import tpu as pltpu
from jax.sharding import Mesh
from jax.sharding import PartitionSpec as P

SEQ = ("yh", "z", "c")
ROW = ("x", "yl")
Y = ("yh", "yl")
BF = jnp.bfloat16
F32 = jnp.float32


def swapped(a, axis):
    return lax.ppermute(a, axis, [(0, 1), (1, 0)])


def along_z(a, sign, cores=(0, 1)):
    n = lax.axis_size("z")
    pairs = [
        (2 * i + c, 2 * ((i + sign * (1 - 2 * c)) % n) + c) for i in range(n) for c in cores
    ]
    return lax.ppermute(a, ("z", "c"), pairs)


def exchanged(pieces, axis):
    return [pieces[0]] + [
        lax.ppermute(pieces[r], axis, [(i, i ^ r) for i in range(4)]) for r in (1, 2, 3)
    ]


def chosen(blocks, index):
    out = blocks[-1]
    for i in range(len(blocks) - 2, -1, -1):
        out = jnp.where(index == i, blocks[i], out)
    return out


def places(core, z, yl):
    sign = 1 - 2 * core
    late = (yl + z + 1) % 2
    one = (z + sign * (1 + late)) % 8
    two = jnp.where(late == 0, z + 3 * sign, z + 4 * (1 - core)) % 8
    return one // 2, two // 2


def rows_of(a, core, z, yl):
    blocks = jnp.split(a, 4, axis=-1)
    return jnp.concatenate([chosen(blocks, p) for p in places(core, z, yl)], axis=-1)


def by_half(a, yh):
    left, right = jnp.split(a, 2, axis=1)
    first = yh == 0
    got = swapped(jnp.where(first, right, left), "yh")
    return jnp.where(first, left, right), got


def whole_columns(a, yh):
    got = swapped(a[1], "yh")
    first = yh == 0
    return jnp.concatenate([jnp.where(first, a[0], got), jnp.where(first, got, a[0])], axis=1)


def reduce_scatter_z(a, place, c):
    early = lax.dynamic_index_in_dim(a, (place + 1) % 2, 0, keepdims=False)
    late = lax.dynamic_index_in_dim(a, place % 2, 0, keepdims=False)
    sent = yield along_z(late[1], 1, (0,))
    for chunk in (early[1], late[0], early[0]):
        sent = yield along_z(sent + chunk, 1)
    mine = jnp.where(c == 0, sent, sent + late[1])
    yield (mine.astype(F32) + swapped(mine, "c").astype(F32)).astype(a.dtype)


def all_gather_z(a, place, c):
    found, last = [], a
    for k in range(4):
        last = yield along_z(last, -1, (0, 1) if k < 3 else (0,))
        found.append(last)
    one, two, three, four = found
    four = jnp.where(c == 0, four, a)
    even = place % 2 == 0
    rows = [
        [jnp.where(even, two, one), jnp.where(even, four, three)],
        [jnp.where(even, one, two), jnp.where(even, three, four)],
    ]
    yield jnp.stack([jnp.stack(r) for r in rows])


def tied(*arrays):
    return lax.optimization_barrier(arrays)


def added(pieces):
    return sum(p.astype(F32) for p in pieces).astype(BF)


def called(body, ins, outs):
    space = pl.BlockSpec(memory_space=pltpu.VMEM)
    return pl.pallas_call(
        body,
        out_shape=[jax.ShapeDtypeStruct(shape, BF) for shape in outs],
        in_specs=[space] * len(ins),
        out_specs=[space] * len(outs),
        compiler_params=pltpu.CompilerParams(vmem_limit_bytes=40 * 2**20),
    )(*ins)


def side_by_side(ref, h):
    return jnp.concatenate([ref[x, h] for x in range(4)], axis=1)


def outer(left, right, factor):
    f, g = left[0].shape[2], right[0].shape[3]

    def body(*refs):
        lefts, rights, out = refs[:4], refs[4:6], refs[6]
        total = [0.0, 0.0]
        for core in range(2):
            for h in range(2):
                wide = side_by_side(rights[core], h)
                for l in range(2):
                    total[l] += lax.dot_general(
                        lefts[2 * h + l][core], wide, (((0,), (0,)), ((), ())),
                        preferred_element_type=F32,
                    )
        for l in range(2):
            done = (total[l] * factor).astype(BF)
            out[l, 0], out[l, 1] = done[: f // 2], done[f // 2 :]

    return called(body, (*left, *right), [(2, 2, f // 2, 4 * g)])[0]


def through(left, middle, g, factor):
    t = left[0].shape[1]

    def body(*refs):
        lefts, mid, outs = refs[:4], refs[4], refs[5:]
        for h in range(2):
            for core in range(2):
                new = sum(
                    jnp.dot(lefts[2 * h + l][core], mid[l], preferred_element_type=F32)
                    for l in range(2)
                )
                new = (new * factor).astype(BF)
                for x in range(4):
                    outs[core][x, h] = new[:, x * g : (x + 1) * g]

    return called(body, (*left, middle), [(4, 2, t, g)] * 2)


def back(right, middle, factor):
    t, f = right[0].shape[2], middle.shape[1]

    def body(*refs):
        rights, mid, outs = refs[:2], refs[2], refs[3:]
        for core in range(2):
            for h in range(2):
                wide = side_by_side(rights[core], h)
                for l in range(2):
                    new = lax.dot_general(
                        wide, mid[l], (((1,), (1,)), ((), ())), preferred_element_type=F32
                    )
                    outs[2 * h + l][core] = (new * factor).astype(BF)

    return called(body, (*right, middle), [(2, t, f)] * 4)


def per_device(context_keys, context_values, question_states, cotangent):
    yh, z, c = (lax.axis_index(a) for a in SEQ)
    yl = lax.axis_index("yl")
    tokens, width = context_keys.shape
    factor = 1.0 / math.sqrt(width * lax.axis_size(ROW) * tokens * lax.axis_size(SEQ))
    half = width // 2
    place = z + yl
    def from_all(a):
        return lax.all_to_all(jnp.broadcast_to(a[None], (4, *a.shape)), "x", 0, 0, tiled=True)

    cot = jnp.stack(by_half(cotangent, yh))

    def for_cores(a):
        return jnp.stack([rows_of(a, c, z, yl), swapped(rows_of(a, 1 - c, z, yl), "c")])

    cot, que = tied(cot, for_cores(question_states))
    right = jnp.stack(by_half(tied(context_values, cot)[0], yh))
    left = for_cores(tied(context_keys, cot)[0])
    cot = from_all(cot)
    que = exchanged([que] * 4, Y)
    key = exchanged([tied(left, que[1])[0]] * 4, Y)
    cot, *que = tied(cot, *que)
    val = from_all(tied(right, cot)[0])
    cot = cot, swapped(cot, "c")

    steps = reduce_scatter_z(outer(que, cot, 1.0), place, c)
    at, *key = tied(next(steps), *key)
    at, val = tied(steps.send(at), val)
    at, other = tied(steps.send(at), swapped(val, "c"))
    val = val, other
    at, adapter = tied(steps.send(at), outer(key, val, factor))
    grad = steps.send(at)

    steps, others = reduce_scatter_z(adapter, place, c), all_gather_z(grad, place, c)
    at, beside = tied(next(steps), next(others))
    for _ in range(3):
        at, beside = tied(steps.send(at), others.send(beside))
    adapter, grad = steps.send(at), others.send(beside).reshape(2, half, 4 * half)

    def cores_summed(own, give):
        return added((own, swapped(give, "c")))

    steps = all_gather_z(adapter, place, c)
    own, give = through(key, grad, half, factor)
    grad, give = tied(grad, give)
    at, own, *part = tied(next(steps), own, *back(val, grad, factor))
    part = exchanged(part, Y)
    values = cores_summed(own, give)
    at = tied(steps.send(at), values)[0]
    values = lax.all_to_all(values, "x", 0, 0, tiled=True)
    at, part[2] = tied(steps.send(at), part[2])
    at, values, part[1], part[3] = tied(steps.send(at), values, part[1], part[3])
    adapter = steps.send(at).reshape(2, half, 4 * half)
    states = cores_summed(*through(que, adapter, half, 1.0))
    part = tied(*part, states)[:4]
    states = lax.all_to_all(states, "x", 0, 0, tiled=True)
    part = added(part)
    grad_values = whole_columns(added(values), yh)

    blocks = jnp.split(part[0], 2, axis=1) + jnp.split(swapped(part[1], "c"), 2, axis=1)
    found = places(c, z, yl) + places(1 - c, z, yl)
    columns = []
    for i in range(4):
        out = blocks[3]
        for j in range(3):
            out = jnp.where(found[j] == i, blocks[j], out)
        columns.append(out)
    grad_keys = jnp.concatenate(columns, axis=1)
    adapted = whole_columns(added(states), yh)
    return adapted, grad_keys, grad_values


def solution(mesh):
    split = Mesh(mesh.devices.reshape(2, 8, 2, 4, 2), SEQ + ROW)
    spec = P(SEQ, ROW)
    return jax.shard_map(
        per_device,
        mesh=split,
        in_specs=(spec, spec, spec, spec),
        out_specs=(spec, spec, spec),
        check_vma=False,
    )
```
